128 devices in a mesh: dom: 64 (over z, y, x_lo, core), edge: 2 (over x_hi).
Axes of the slice: x: 4 (x_hi: 2, x_lo: 2; x = x_hi * 2 + x_lo), y: 4, z: 4, core: 2. Of those that a mesh axis runs over, the one named last changes fastest.
Arguments:
- src_emb: float32 [65536, 400], P(('dom', 'edge')), may hold values from -1.8 to 1.8
- src_acc: float32 [65536], P(('dom', 'edge')), may hold values from 0.1 to 2
- dst_emb: float32 [65536, 400], P('dom'), may hold values from -1.8 to 1.8
- dst_acc: float32 [65536], P('dom'), may hold values from 0.1 to 2
- relations: float32 [32, 400], replicated, may hold values from 0.25 to 1.75
- rel_acc: float32 [32], replicated, may hold values from 0.00534578 to 0.0534578
- edge_src: int32 [64, 2, 3, 1536], P('dom', 'edge'), may hold values from 0 to 511
- edge_dst: int32 [64, 2, 3, 1536], P('dom', 'edge'), may hold values from 0 to 1023
- edge_rel: int32 [64, 2, 3, 1536], P('dom', 'edge'), may hold values from 0 to 31
- edge_counts: int32 [64, 2, 3], P('dom', 'edge'), may hold values from 512 to 1536, as said below
- neg_dst: int32 [64, 2, 3, 2, 1024], P('dom', 'edge'), may hold values from 0 to 1023
Outputs:
- src_out: float32 [65536, 400], P(('dom', 'edge'))
- src_acc_out: float32 [65536], P(('dom', 'edge'))
- dst_out: float32 [65536, 400], P('dom')
- dst_acc_out: float32 [65536], P('dom')
- rel_out: float32 [32, 400], replicated
The draws below stay inside these ranges and needn't reach their ends.
Inputs may be any that keep to these rules, and one draw needn't show every extreme that they name: Live edges fill the first edge_counts slots of their split; every draw has a split with 1536 live edges and one with 512.
All inputs are finite; a program needn't handle non-finite values.
Results may differ from the reference program's by a relative error of at most 0.0003.
Values sent between devices are 32-bit elements; how exact they have to be, the bound alone decides.
No kernel may reach another device: no remote copies, remote signals or barrier semaphores. Data moves between devices by JAX's collectives and lax.ppermute only.
A program may use at most 128 MiB of HBM per device.

```python
import math
import jax
import jax.numpy as jnp
from jax import lax

D = 400
ROWS = 1024
NEG = 1024
GROUPS = 2
ROUNDS = 3
RELS = 32
PARTS_SIZE = 64
SPLITS = 2
HALF = 512
CAP = 1536
REL_EDGES = 18432


def table_scale(key):
    column_key = jax.random.fold_in(key, 0)
    table_rows = PARTS_SIZE * ROWS
    partition_idx = (jnp.arange(table_rows, dtype=jnp.int32) // ROWS).astype(jnp.float32)
    growth = 1.5 ** (partition_idx / max(PARTS_SIZE - 1, 1))
    column_factor = jax.random.uniform(column_key, (PARTS_SIZE, D), jnp.float32, 0.6, 1.5)
    column_factor = jnp.repeat(column_factor, ROWS, axis=0)
    return 0.24 * growth[:, None] * column_factor


def draw_src_emb(key, part):
    key = jax.random.fold_in(key, 11)
    noise_key, scale_key = jax.random.split(key)
    noise = jax.random.truncated_normal(noise_key, -3.0, 3.0, (PARTS_SIZE * ROWS, D), jnp.float32)
    result = noise * table_scale(scale_key)
    return result


def draw_dst_emb(key, part):
    key = jax.random.fold_in(key, 12)
    noise_key, scale_key = jax.random.split(key)
    noise = jax.random.truncated_normal(noise_key, -3.0, 3.0, (PARTS_SIZE * ROWS, D), jnp.float32)
    result = noise * table_scale(scale_key)
    return result


def draw_edge_rel(key, part):
    key = jax.random.fold_in(key, 13)
    perm_key, level_key = jax.random.split(key)
    workers = PARTS_SIZE * SPLITS
    orders = jax.vmap(lambda single: jax.random.permutation(single, RELS))(jax.random.split(perm_key, workers))
    levels = jax.random.randint(level_key, (workers, ROUNDS * CAP), 0, 64)
    ranks = (RELS * levels * levels // 4096).astype(jnp.int32)
    picked = jnp.take_along_axis(orders.astype(jnp.int32), ranks, axis=1)
    return picked.reshape(PARTS_SIZE, SPLITS, ROUNDS, CAP).astype(jnp.int32)


def draw_edge_counts(key, part):
    key = jax.random.fold_in(key, 7)
    first_key, second_key = jax.random.split(key)
    lowest = CAP // 3
    levels = jax.random.randint(first_key, (PARTS_SIZE * SPLITS * ROUNDS,), 0, 65)
    counts = lowest + (CAP - lowest) * levels * levels // 4096
    picks = jax.random.permutation(second_key, PARTS_SIZE * SPLITS * ROUNDS)
    counts = counts.at[picks[0]].set(CAP).at[picks[1]].set(lowest)
    return counts.reshape(PARTS_SIZE, SPLITS, ROUNDS).astype(jnp.int32)


def plant(values, stream_key, low, top_value):
    shape = values.shape
    index_at = [jax.random.randint(jax.random.fold_in(stream_key, axis), (), 0, shape[axis]) for axis in range(len(shape))]
    values = values.at[tuple(index_at)].set(low)
    longest = shape.index(max(shape))
    index_at[longest] = (index_at[longest] + 1) % shape[longest]
    return values.at[tuple(index_at)].set(top_value)


def level_of(key, shape, shards, smallest, largest):
    def one(position, shards_of):
        steps = jax.random.uniform(jax.random.fold_in(jax.random.fold_in(key, 6), position), (shards_of,), jnp.float32, smallest / len(shards), largest / len(shards))
        return jnp.repeat(jnp.exp(steps), shape[position] // shards_of).reshape((-1,) + (1,) * (len(shape) - position - 1))

    level = one(*shards[0])
    for cut in shards[1:]:
        level = level * one(*cut)
    return level


def setup_inputs(seed: int = 0) -> dict:
    keys = jax.random.split(jax.random.key(seed), 12)
    src_emb = draw_src_emb(jax.random.fold_in(keys[11], 71), 0)
    src_acc = jnp.clip(jnp.exp(math.log(2.0) - 2.9957323 * jax.random.uniform(keys[1], (PARTS_SIZE * ROWS,), jnp.float32) ** level_of(keys[1], (PARTS_SIZE * ROWS,), ((0, 128),), -0.2, 0.2)), 0.1, 2.0)
    dst_emb = draw_dst_emb(jax.random.fold_in(keys[11], 71), 0)
    dst_acc = jnp.clip(jnp.exp(math.log(2.0) - 2.9957323 * jax.random.uniform(keys[3], (PARTS_SIZE * ROWS,), jnp.float32) ** level_of(keys[3], (PARTS_SIZE * ROWS,), ((0, 64),), -0.2, 0.2)), 0.1, 2.0)
    relations = jnp.clip(1.0 + 0.15 * jax.random.normal(keys[4], (RELS, D), jnp.float32), 0.25, 1.75)
    rel_acc = jnp.clip(jnp.exp(jax.random.uniform(keys[5], (RELS,), jnp.float32, math.log(0.00534578), math.log(0.0534578))), 0.00534578, 0.0534578)
    edge_src = plant(jax.random.randint(keys[6], (PARTS_SIZE, SPLITS, ROUNDS, CAP), 0, HALF), jax.random.fold_in(keys[6], 1), 0, HALF - 1).astype(jnp.int32)
    edge_dst = plant(jax.random.randint(keys[7], (PARTS_SIZE, SPLITS, ROUNDS, CAP), 0, ROWS), jax.random.fold_in(keys[7], 1), 0, ROWS - 1).astype(jnp.int32)
    edge_rel = draw_edge_rel(jax.random.fold_in(keys[11], 71), 0)
    edge_counts = draw_edge_counts(jax.random.fold_in(keys[11], 71), 0)
    neg_dst = plant(jax.random.randint(keys[10], (PARTS_SIZE, SPLITS, ROUNDS, GROUPS, NEG), 0, ROWS), jax.random.fold_in(keys[10], 1), 0, ROWS - 1).astype(jnp.int32)
    return {"src_emb": src_emb, "src_acc": src_acc, "dst_emb": dst_emb, "dst_acc": dst_acc, "relations": relations, "rel_acc": rel_acc, "edge_src": edge_src, "edge_dst": edge_dst, "edge_rel": edge_rel, "edge_counts": edge_counts, "neg_dst": neg_dst}


LEARN_RATE = 0.2
REL_RATE = 0.3
NEG_WEIGHT = 0.1
HIGH = lax.Precision.HIGHEST

def group_terms(src_rows, dst_rows, relations, src_pick, dst_pick, rel_pick, neg_pick, live_mask):
    sources = jnp.take(src_rows, src_pick, axis=0)
    targets = jnp.take(dst_rows, dst_pick, axis=0)
    onehot = (rel_pick[:, None] == jnp.arange(relations.shape[0], dtype=jnp.int32)[None, :]).astype(jnp.float32)
    diagonal = jnp.dot(onehot, relations, precision=HIGH, preferred_element_type=jnp.float32)
    queries = sources * diagonal
    positive = lax.optimization_barrier(jnp.sum(queries * targets, axis=1))
    negatives = jnp.take(dst_rows, neg_pick, axis=0)
    scores = lax.dot_general(queries, negatives, (((1,), (1,)), ((), ())), precision=HIGH, preferred_element_type=jnp.float32)
    pos_grad = -jax.nn.sigmoid(-positive) * live_mask
    neg_grad = NEG_WEIGHT * jax.nn.sigmoid(scores) * live_mask[:, None]
    query_grad = pos_grad[:, None] * targets + jnp.dot(neg_grad, negatives, precision=HIGH, preferred_element_type=jnp.float32)
    target_grad = pos_grad[:, None] * queries
    negative_grad = lax.dot_general(neg_grad, queries, (((0,), (0,)), ((), ())), precision=HIGH, preferred_element_type=jnp.float32)
    source_grad = query_grad * diagonal
    relation_grad = lax.dot_general(onehot, query_grad * sources, (((0,), (0,)), ((), ())), precision=HIGH, preferred_element_type=jnp.float32)
    return (source_grad, target_grad, negative_grad, relation_grad)

def bucket_grads(src_rows, dst_rows, relations, src_list, dst_list, rel_list, neg_lists, live_count, group_stop):
    group_len = src_list.shape[0] // neg_lists.shape[0]

    def one_group(group_idx, totals):
        src_total, dst_total, rel_total = totals
        offset = (group_idx * group_len).astype(jnp.int32)
        src_pick = lax.dynamic_slice_in_dim(src_list, offset, group_len)
        dst_pick = lax.dynamic_slice_in_dim(dst_list, offset, group_len)
        rel_pick = lax.dynamic_slice_in_dim(rel_list, offset, group_len)
        neg_pick = lax.dynamic_index_in_dim(neg_lists, offset // group_len, 0, keepdims=False)
        positions = offset + jnp.arange(group_len, dtype=jnp.int32)
        live_mask = (positions < live_count).astype(jnp.float32)
        source_grad, target_grad, negative_grad, relation_grad = group_terms(src_rows, dst_rows, relations, src_pick, dst_pick, rel_pick, neg_pick, live_mask)
        src_total = src_total.at[src_pick].add(source_grad)
        dst_total = dst_total.at[dst_pick].add(target_grad).at[neg_pick].add(negative_grad)
        return (src_total, dst_total, rel_total + relation_grad)
    totals = (jnp.zeros(src_rows.shape, jnp.float32), jnp.zeros(dst_rows.shape, jnp.float32), jnp.zeros(relations.shape, jnp.float32))
    return lax.fori_loop(jnp.int32(0), group_stop, one_group, totals)

def adagrad_rows(table, state, grad, rate):
    new_state = state + lax.optimization_barrier(jnp.mean(grad * grad, axis=-1))
    return (table - rate * grad / jnp.sqrt(new_state)[..., None], new_state)

def reference(src_emb, src_acc, dst_emb, dst_acc, relations, rel_acc, edge_src, edge_dst, edge_rel, edge_counts, neg_dst):
    src_parts = src_emb.reshape(PARTS_SIZE * SPLITS, HALF, D)
    src_state = src_acc.reshape(PARTS_SIZE * SPLITS, HALF)
    held = dst_emb.reshape(PARTS_SIZE, ROWS, D)
    held_state = dst_acc.reshape(PARTS_SIZE, ROWS)
    rel_total = jnp.zeros((RELS, D), jnp.float32)
    workers = jnp.arange(PARTS_SIZE * SPLITS, dtype=jnp.int32)
    for round_idx in range(ROUNDS):

        def worker_grads(worker):
            part = worker // SPLITS
            split = worker % SPLITS
            return bucket_grads(src_parts[worker], held[part], relations, edge_src[part, split, round_idx], edge_dst[part, split, round_idx], edge_rel[part, split, round_idx], neg_dst[part, split, round_idx], edge_counts[part, split, round_idx], jnp.int32(GROUPS))
        src_grad, dst_grad, rel_grad = lax.map(worker_grads, workers)
        dst_grad = lax.optimization_barrier(jnp.sum(dst_grad.reshape(PARTS_SIZE, SPLITS, ROWS, D), axis=1))
        src_parts, src_state = adagrad_rows(src_parts, src_state, src_grad, LEARN_RATE)
        held, held_state = adagrad_rows(held, held_state, dst_grad, LEARN_RATE)
        held = jnp.roll(held, 1, axis=0)
        held_state = jnp.roll(held_state, 1, axis=0)
        rel_total = rel_total + lax.optimization_barrier(jnp.sum(rel_grad, axis=0))
    rel_mean = rel_total / REL_EDGES
    rel_scale = jnp.sqrt(rel_acc + lax.optimization_barrier(jnp.mean(rel_mean * rel_mean, axis=1)))
    rel_out = relations - REL_RATE * rel_mean / rel_scale[:, None]
    return (src_parts.reshape(PARTS_SIZE * ROWS, D), src_state.reshape(PARTS_SIZE * ROWS), held.reshape(PARTS_SIZE * ROWS, D), held_state.reshape(PARTS_SIZE * ROWS), rel_out)
```

```python
import functools

import jax
import jax.numpy as jnp
from jax import lax
from jax.experimental import pallas as pl
from jax.experimental.pallas import tpu as pltpu
from jax.sharding import PartitionSpec as P

LEARN_RATE = 0.2
REL_RATE = 0.3
NEG_WEIGHT = 0.1
TILE = 256
PAD = 8
LANES = 128
BF = jnp.bfloat16
F32 = jnp.float32
AXES = ("dom", "edge")
NN = (((1,), (0,)), ((), ()))
NT = (((1,), (1,)), ((), ()))


def mm(a, b, dims=NN):
    return lax.dot_general(a, b, dims, preferred_element_type=F32)


def split(x):
    hi = x.astype(BF)
    return hi, (x - hi.astype(F32)).astype(BF)


def iota(shape, dim):
    return lax.broadcasted_iota(jnp.int32, shape, dim)


def hot(cond):
    return jnp.where(cond, F32(1), F32(0)).astype(BF)


def mult_kernel(neg_ref, out_ref):
    rows = out_ref.shape[1]
    high = rows // 32
    for c in range(neg_ref.shape[0]):
        neg = neg_ref[c : c + 1, :]
        count = neg.shape[1]
        hot_hi = hot(iota((high, count), 0) == (neg >> 5))
        hot_lo = hot(iota((32, count), 0) == (neg & 31))
        counts_hi, counts_lo = split(mm(hot_hi, hot_lo, NT))
        pick = hot(iota((rows, high), 1) == (iota((rows, high), 0) >> 5))
        mask = iota((rows, 32), 1) == (iota((rows, 32), 0) & 31)
        ones = jnp.ones((32, LANES), BF)
        total = jnp.zeros((rows, LANES), F32)
        for part in (counts_hi, counts_lo):
            total += mm(jnp.where(mask, mm(pick, part), F32(0)).astype(BF), ones)
        out_ref[c] = total * NEG_WEIGHT


def multiplicity(neg, rows):
    return pl.pallas_call(
        mult_kernel,
        out_shape=jax.ShapeDtypeStruct((neg.shape[0], rows, LANES), F32),
        cost_estimate=pl.CostEstimate(flops=10**9, bytes_accessed=10**6, transcendentals=0),
        name="multiplicity",
    )(neg)


def updated(table, state, grad):
    width = table.shape[0]
    new_state = state + jnp.sum(grad * grad, axis=0, keepdims=True) * F32(1.0 / width)
    return table - LEARN_RATE * grad / jnp.sqrt(new_state), new_state


def packed(dim, table, state):
    return jnp.concatenate([table, jnp.broadcast_to(state, (PAD, state.shape[1]))], axis=0)


def edge_kernel(
    fresh,
    count_ref,
    es_ref,
    ed_ref,
    er_ref,
    mult_ref,
    src_ref,
    dst_ref,
    rel_ref,
    relsum_ref,
    *rest,
):
    if not fresh:
        mine_ref, other_ref, *rest = rest
    src_out, q_out, whi_out, wlo_out, relsum_out, *rest = rest
    if not fresh:
        dst_out, *rest = rest
    s2, r2, t2, tcat, gsrc, grel = rest
    step = pl.program_id(0)
    width = s2.shape[0] // 2
    rows = t2.shape[1]
    halves = s2.shape[1]
    rels = r2.shape[1]

    @pl.when(step == 0)
    def _():
        dst = dst_ref[:width, :]
        if not fresh:
            grad = mine_ref[...] + other_ref[...]
            dst, state = updated(dst, dst_ref[width : width + 1, :], grad)
            dst_out[...] = packed(width, dst, state)
        thi, tlo = split(dst)
        t2[:width, :] = thi
        t2[width:, :] = tlo
        tcat[...] = jnp.concatenate([thi, thi, tlo], axis=0).T
        shi, slo = split(src_ref[:width, :])
        s2[:width, :] = shi
        s2[width:, :] = slo
        rhi, rlo = split(rel_ref[...])
        r2[:width, :] = rhi
        r2[width:, :] = rlo
        gsrc[...] = jnp.zeros_like(gsrc)
        grel[...] = jnp.zeros_like(grel)

    @pl.when(step * TILE < count_ref[0])
    def _():
        at = hot(iota((halves, TILE), 0) == es_ref[...])
        bt = hot(iota((rels, TILE), 0) == er_ref[...])
        both = mm(s2[...], at)
        sources = both[:width] + both[width:]
        both = mm(r2[...], bt)
        diag = both[:width] + both[width:]
        query = sources * diag
        qhi, qlo = split(query)
        q_out[:width, :] = qhi
        q_out[width:, :] = qlo
        scores = mm(tcat[...], jnp.concatenate([qhi, qlo, qhi], axis=0))
        live = jnp.where(iota((1, TILE), 1) + step * TILE < count_ref[0], F32(1), F32(0))
        mult = mult_ref[...].reshape(rows, LANES)
        mult = jnp.concatenate([mult] * (TILE // LANES), axis=1)
        named = jnp.where(iota((rows, TILE), 0) == ed_ref[...], F32(1), F32(0))
        weights = (jax.nn.sigmoid(scores) * (mult + named) - named) * live
        whi, wlo = split(weights)
        whi_out[...] = whi
        wlo_out[...] = wlo
        both = mm(t2[...], whi)
        qgrad = both[:width] + both[width:] + mm(t2[:width, :], wlo)
        hi, lo = split(qgrad * diag)
        gsrc[...] += mm(jnp.concatenate([hi, lo], axis=0), at, NT)
        hi, lo = split(qgrad * sources)
        grel[...] += mm(jnp.concatenate([hi, lo], axis=0), bt, NT)

    @pl.when(step == pl.num_programs(0) - 1)
    def _():
        grad = gsrc[:width, :] + gsrc[width:, :]
        table, state = updated(src_ref[:width, :], src_ref[width : width + 1, :], grad)
        src_out[...] = packed(width, table, state)
        relsum_out[...] = relsum_ref[...] + (grel[:width, :] + grel[width:, :]).T


def edge_pass(count, lists, mult, src, dst, rel, relsum, grads=None):
    fresh = grads is None
    slots = lists.shape[1]
    tiles = slots // TILE
    per = tiles // mult.shape[0]
    width = rel.shape[0]
    rows, halves = dst.shape[1], src.shape[1]

    def whole(shape):
        return pl.BlockSpec(shape, lambda i: (0,) * len(shape))

    def listed(k):
        return pl.BlockSpec((None, 1, TILE), lambda i, k=k: (k, 0, i))

    lists3 = lists[:, None, :]
    operands = [count, lists3, lists3, lists3, mult, src, dst, rel, relsum]
    in_specs = [
        pl.BlockSpec(memory_space=pltpu.SMEM),
        listed(0),
        listed(1),
        listed(2),
        pl.BlockSpec((1, rows, LANES), lambda i: (i // per, 0, 0)),
        whole(src.shape),
        whole(dst.shape),
        whole(rel.shape),
        whole(relsum.shape),
    ]
    out_shape = [
        jax.ShapeDtypeStruct(src.shape, F32),
        jax.ShapeDtypeStruct((2 * width, slots), BF),
        jax.ShapeDtypeStruct((rows, slots), BF),
        jax.ShapeDtypeStruct((rows, slots), BF),
        jax.ShapeDtypeStruct(relsum.shape, F32),
    ]
    out_specs = [
        whole(src.shape),
        pl.BlockSpec((2 * width, TILE), lambda i: (0, i)),
        pl.BlockSpec((rows, TILE), lambda i: (0, i)),
        pl.BlockSpec((rows, TILE), lambda i: (0, i)),
        whole(relsum.shape),
    ]
    if not fresh:
        operands += list(grads)
        in_specs += [whole(grads[0].shape)] * 2
        out_shape.append(jax.ShapeDtypeStruct(dst.shape, F32))
        out_specs.append(whole(dst.shape))
    return pl.pallas_call(
        functools.partial(edge_kernel, fresh),
        grid=(tiles,),
        in_specs=in_specs,
        out_specs=out_specs,
        out_shape=out_shape,
        scratch_shapes=[
            pltpu.VMEM((2 * width, halves), BF),
            pltpu.VMEM((2 * width, rel.shape[1]), BF),
            pltpu.VMEM((2 * width, rows), BF),
            pltpu.VMEM((rows, 3 * width), BF),
            pltpu.VMEM((2 * width, halves), F32),
            pltpu.VMEM((2 * width, rel.shape[1]), F32),
        ],
        compiler_params=pltpu.CompilerParams(vmem_limit_bytes=48 * 2**20),
        cost_estimate=pl.CostEstimate(flops=14 * 10**9, bytes_accessed=10**7, transcendentals=10**6),
        name="edge_pass",
    )(*operands)


def dst_kernel(count_ref, q_ref, whi_ref, wlo_ref, out_ref):
    step = pl.program_id(0)
    width = out_ref.shape[0]

    @pl.when(step == 0)
    def _():
        out_ref[...] = jnp.zeros_like(out_ref)

    @pl.when(step * TILE < count_ref[0])
    def _():
        both = mm(q_ref[...], whi_ref[...], NT)
        out_ref[...] += both[:width] + both[width:] + mm(q_ref[:width, :], wlo_ref[...], NT)


def dst_pass(count, q, whi, wlo):
    width, (rows, slots) = q.shape[0] // 2, whi.shape
    return pl.pallas_call(
        dst_kernel,
        grid=(slots // TILE,),
        in_specs=[
            pl.BlockSpec(memory_space=pltpu.SMEM),
            pl.BlockSpec((2 * width, TILE), lambda i: (0, i)),
            pl.BlockSpec((rows, TILE), lambda i: (0, i)),
            pl.BlockSpec((rows, TILE), lambda i: (0, i)),
        ],
        out_specs=pl.BlockSpec((width, rows), lambda i: (0, 0)),
        out_shape=jax.ShapeDtypeStruct((width, rows), F32),
        compiler_params=pltpu.CompilerParams(vmem_limit_bytes=48 * 2**20),
        cost_estimate=pl.CostEstimate(flops=5 * 10**9, bytes_accessed=10**7, transcendentals=0),
        name="dst_pass",
    )(count, q, whi, wlo)


def update_kernel(dst_ref, mine_ref, other_ref, out_ref):
    width = mine_ref.shape[0]
    grad = mine_ref[...] + other_ref[...]
    table, state = updated(dst_ref[:width, :], dst_ref[width : width + 1, :], grad)
    out_ref[...] = packed(width, table, state)


def final_update(dst, mine, other):
    return pl.pallas_call(
        update_kernel,
        out_shape=jax.ShapeDtypeStruct(dst.shape, F32),
        cost_estimate=pl.CostEstimate(flops=10**7, bytes_accessed=10**7, transcendentals=0),
        name="final_update",
    )(dst, mine, other)


def home(p, h, parts):
    return 2 * (p % parts) + h


def place(q, h, parts):
    q = q % parts
    return 2 * (2 * (q // 2) + h) + q % 2


def moved(value, pairs):
    return lax.ppermute(value, AXES, pairs)


def summed_everywhere(value, parts):
    size = 2 * parts
    bit = 1
    while bit < size:
        wide = 2 if bit * 2 < size and bit not in (2,) else 1
        if wide == 2:
            got = [moved(value, [(i, i ^ (k * bit)) for i in range(size)]) for k in (1, 2, 3)]
            value = (value + got[0]) + (got[1] + got[2])
            bit *= 4
        else:
            value = value + moved(value, [(i, i ^ bit) for i in range(size)])
            bit *= 2
    return value


def body(
    src_emb, src_acc, dst_emb, dst_acc, relations, rel_acc, edge_src, edge_dst, edge_rel, edge_counts, neg_dst
):
    parts = lax.axis_size("dom")
    rounds, slots = edge_src.shape[2:]
    blocks = neg_dst.shape[3]
    rows, halves = dst_emb.shape[0], src_emb.shape[0]
    rel_edges = rounds * parts * 2 * slots // relations.shape[0]
    flat = [(p, h) for p in range(parts) for h in range(2)]
    low = 2 * (lax.axis_index("dom") % 2) + lax.axis_index("edge")

    src = packed(None, src_emb.T, src_acc[None, :])
    dst = packed(None, dst_emb.T, dst_acc[None, :])
    src_pairs = [(home(p, h, parts), place(p, h, parts)) for p, h in flat if (p + h) % 2]
    dst_pairs = [(home(q, q % 2, parts), place(q, 1 - q % 2, parts)) for q in range(parts)]
    away = (low == 1) | (low == 2)
    src = jnp.where(away, moved(src, src_pairs), src)
    dst = jnp.where(away, moved(dst, dst_pairs), dst)

    lists = []
    for r in range(rounds):
        mix = jnp.concatenate(
            [
                edge_src[0, 0, r],
                edge_dst[0, 0, r],
                edge_rel[0, 0, r],
                neg_dst[0, 0, r].reshape(-1),
                jnp.broadcast_to(edge_counts[0, 0, r], (LANES,)),
            ]
        )
        lists.append(moved(mix, [(home(p, h, parts), place(p - r, h, parts)) for p, h in flat]))

    relsum = jnp.zeros(relations.shape, F32)
    grads = None
    for r in range(rounds):
        mix = lists[r]
        trio = mix[: 3 * slots].reshape(3, slots)
        negs = mix[3 * slots : 3 * slots + neg_dst.shape[3] * neg_dst.shape[4]].reshape(blocks, -1)
        count = mix[-LANES:][:1]
        mult = multiplicity(negs, rows)
        out = edge_pass(count, trio, mult, src, dst, relations.T, relsum, grads)
        src, q, whi, wlo, relsum = out[:5]
        if grads is not None:
            dst = out[5]
        if r < rounds - 1:
            src = moved(src, [(place(p - r, h, parts), place(p - r - 1, h, parts)) for p, h in flat])
        else:
            src = moved(src, [(place(p - r, h, parts), home(p, h, parts)) for p, h in flat])
        mine = dst_pass(count, q, whi, wlo)
        other = moved(mine, [(place(q, h, parts), place(q, 1 - h, parts)) for q, h in flat])
        grads = (mine, other)
    dst = final_update(dst, *grads)
    dst = moved(dst, [(place(q, h, parts), home(q + rounds, h, parts)) for q, h in flat])

    rel_mean = summed_everywhere(relsum, parts) / rel_edges
    rel_scale = jnp.sqrt(rel_acc + jnp.mean(rel_mean * rel_mean, axis=1))
    rel_out = relations - REL_RATE * rel_mean / rel_scale[:, None]
    width = relations.shape[1]
    return (src[:width].T, src[width], dst[:width].T, dst[width], rel_out)


def solution(mesh):
    return jax.shard_map(
        body,
        mesh=mesh,
        in_specs=(
            P(("dom", "edge"), None),
            P(("dom", "edge")),
            P("dom", None),
            P("dom"),
            P(),
            P(),
            P("dom", "edge", None, None),
            P("dom", "edge", None, None),
            P("dom", "edge", None, None),
            P("dom", "edge", None),
            P("dom", "edge", None, None, None),
        ),
        out_specs=(P(("dom", "edge"), None), P(("dom", "edge")), P("dom", None), P("dom"), P()),
        check_vma=False,
    )
```

```python
import functools

import jax
import jax.numpy as jnp
from jax import lax
from jax.experimental import pallas as pl
from jax.experimental.pallas import tpu as pltpu
from jax.sharding import PartitionSpec as P

LEARN_RATE = 0.2
REL_RATE = 0.3
NEG_WEIGHT = 0.1
TILE = 256
PAD = 8
VMEM_BYTES = 48 * 2**20
LANES = 128
BF = jnp.bfloat16
F32 = jnp.float32
CHEAP = pl.CostEstimate(flops=10**6, bytes_accessed=10**5, transcendentals=0)
AXES = ("dom", "edge")
NN = (((1,), (0,)), ((), ()))
NT = (((1,), (1,)), ((), ()))


def mm(a, b, dims=NN):
    return lax.dot_general(a, b, dims, preferred_element_type=F32)


def split(x):
    hi = x.astype(BF)
    return hi, (x - hi.astype(F32)).astype(BF)


def iota(shape, dim):
    return lax.broadcasted_iota(jnp.int32, shape, dim)


def hot(cond):
    return jnp.where(cond, F32(1), F32(0)).astype(BF)


def pack_kernel(count_ref, es_ref, ed_ref, er_ref, neg_ref, acc_ref, *outs):
    for r, out_ref in enumerate(outs):
        parts = [es_ref[r], ed_ref[r], er_ref[r]] + [neg_ref[r, c : c + 1, :] for c in range(neg_ref.shape[1])]
        parts = [part.astype(F32) for part in parts] + [acc_ref[...]]
        parts.append(jnp.full((1, LANES), count_ref[0, r], jnp.int32).astype(F32))
        out_ref[...] = jnp.concatenate(parts, axis=1)


def packed_lists(edge_src, edge_dst, edge_rel, counts, neg_dst, src_acc):
    rounds, slots = edge_src.shape[2:]
    size = 3 * slots + neg_dst.shape[3] * neg_dst.shape[4] + src_acc.shape[0] + LANES
    return pl.pallas_call(
        pack_kernel,
        in_specs=[pl.BlockSpec(memory_space=pltpu.SMEM)] + [pl.BlockSpec(memory_space=pltpu.VMEM)] * 5,
        out_shape=[jax.ShapeDtypeStruct((1, size), F32)] * rounds,
        cost_estimate=CHEAP,
        name="pack_lists",
    )(
        counts.reshape(1, rounds),
        edge_src.reshape(rounds, 1, slots),
        edge_dst.reshape(rounds, 1, slots),
        edge_rel.reshape(rounds, 1, slots),
        neg_dst.reshape(neg_dst.shape[2:]),
        src_acc.reshape(1, -1),
    )


def mult_kernel(start, mix_ref, out_ref):
    rows = out_ref.shape[1]
    high = rows // 32
    count = rows
    for c in range(out_ref.shape[0]):
        neg = mix_ref[:, start + c * count : start + (c + 1) * count].astype(jnp.int32)
        hot_hi = hot(iota((high, count), 0) == (neg >> 5))
        hot_lo = hot(iota((32, count), 0) == (neg & 31))
        counts_hi, counts_lo = split(mm(hot_hi, hot_lo, NT))
        pick = hot(iota((rows, high), 1) == (iota((rows, high), 0) >> 5))
        mask = iota((rows, 32), 1) == (iota((rows, 32), 0) & 31)
        ones = jnp.ones((32, LANES), BF)
        total = jnp.zeros((rows, LANES), F32)
        for part in (counts_hi, counts_lo):
            total += mm(jnp.where(mask, mm(pick, part), F32(0)).astype(BF), ones)
        out_ref[c] = total * (0.5 * NEG_WEIGHT)


def multiplicity(mix, start, blocks, rows):
    return pl.pallas_call(
        functools.partial(mult_kernel, start),
        out_shape=jax.ShapeDtypeStruct((blocks, rows, LANES), F32),
        cost_estimate=CHEAP,
        name="multiplicity",
    )(mix)


def updated(table, state, grad):
    width = table.shape[0]
    new_state = state + jnp.sum(grad * grad, axis=0, keepdims=True) * F32(1.0 / width)
    return table - LEARN_RATE * grad / jnp.sqrt(new_state), new_state


def prep_kernel(fresh, *refs):
    if fresh:
        away_ref, dst_ref, other_dst_ref, state_ref, other_state_ref, t3, tcat, dst_out, state_out = refs
        away = away_ref[0] > 0
        dst = jnp.where(away, other_dst_ref[...], dst_ref[...])
        state = jnp.where(away, other_state_ref[...], state_ref[...])
    else:
        dst_ref, state_ref, mine_ref, other_ref, t3, tcat, dst_out, state_out = refs
        dst, state = updated(dst_ref[...], state_ref[...], mine_ref[...] + other_ref[...])
    dst_out[...] = dst
    state_out[...] = state
    thi, tlo = split(dst)
    t3[...] = jnp.concatenate([thi, tlo, thi], axis=1)
    thi, tlo = thi * BF(0.5), tlo * BF(0.5)
    tcat[...] = jnp.concatenate([thi, thi, tlo], axis=0).T


def prepared(fresh, *operands):
    width, rows = operands[1].shape if fresh else operands[0].shape
    specs = [pl.BlockSpec(memory_space=pltpu.VMEM)] * len(operands)
    if fresh:
        specs[0] = pl.BlockSpec(memory_space=pltpu.SMEM)
    return pl.pallas_call(
        functools.partial(prep_kernel, fresh),
        in_specs=specs,
        out_shape=[
            jax.ShapeDtypeStruct((width, 3 * rows), BF),
            jax.ShapeDtypeStruct((rows, 3 * width), BF),
            jax.ShapeDtypeStruct((width, rows), F32),
            jax.ShapeDtypeStruct((1, rows), F32),
        ],
        cost_estimate=CHEAP,
        name="prepare_dst",
    )(*operands)


def edge_kernel(
    fresh,
    final,
    count_ref,
    es_ref,
    ed_ref,
    er_ref,
    acc_ref,
    mult_ref,
    src_ref,
    t3,
    tcat,
    rel_ref,
    relsum_ref,
    gdst,
    relsum_out,
    src_out,
    s2,
    r2,
    gsrc,
    grel,
    live_count,
):
    step = pl.program_id(0)
    width, rows = t3.shape[0], gdst.shape[1]
    halves = gsrc.shape[1]
    rels = r2.shape[1] // 2

    @pl.when(step == 0)
    def _():
        live_count[0] = jnp.max(count_ref[...]).astype(jnp.int32)
        s2[...] = jnp.concatenate(split(src_ref[:width, :]), axis=1)
        r2[...] = jnp.concatenate(split(rel_ref[...]), axis=0).T
        gsrc[...] = jnp.zeros_like(gsrc)
        gdst[...] = jnp.zeros_like(gdst)
        grel[...] = jnp.zeros_like(grel)

    @pl.when(step * TILE < live_count[0])
    def _():
        live = iota((1, TILE), 1) + step * TILE < live_count[0]
        es = jnp.where(live, es_ref[...].astype(jnp.int32), -1)
        er = jnp.where(live, er_ref[...].astype(jnp.int32), -1)
        at = hot(iota((halves, TILE), 0) == es)
        bt = hot(iota((rels, TILE), 0) == er)
        sources = mm(s2[...], jnp.concatenate([at, at], axis=0))
        diag = mm(r2[...], jnp.concatenate([bt, bt], axis=0))
        qhi, qlo = split(sources * diag)
        qcat = jnp.concatenate([qhi, qlo, qhi], axis=0)
        ed = ed_ref[...].astype(jnp.int32)
        pieces = []
        for row in range(0, rows, TILE):
            half = jnp.tanh(mm(tcat[row : row + TILE, :], qcat))
            mult = jnp.concatenate([mult_ref[0, row : row + TILE, :]] * (TILE // LANES), axis=1)
            named = jnp.where(iota((TILE, TILE), 0) + row == ed, F32(0.5), F32(0))
            pieces.append(split(half * (mult + named) + (mult - named)))
        whi, wlo = (jnp.concatenate(piece, axis=0) for piece in zip(*pieces))
        qgrad = mm(t3[...], jnp.concatenate([whi, whi, wlo], axis=0))
        gdst[:width, :] += mm(
            jnp.concatenate([qhi, qlo, qhi], axis=1), jnp.concatenate([whi, whi, wlo], axis=1), NT
        )
        gsrc[...] += mm(
            jnp.concatenate(split(qgrad * diag), axis=1), jnp.concatenate([at, at], axis=1), NT
        )
        grel[...] += mm(
            jnp.concatenate(split(qgrad * sources), axis=1), jnp.concatenate([bt, bt], axis=1), NT
        )

    @pl.when(step == pl.num_programs(0) - 1)
    def _():
        state = acc_ref[...] if fresh else src_ref[width : width + 1, :]
        table, state = updated(src_ref[:width, :], state, gsrc[...])
        src_out[:width, :] = table
        src_out[width:, :] = jnp.broadcast_to(state, (PAD, halves))
        total = relsum_ref[...] + grel[...].T
        relsum_out[...] = total
        if final:
            gdst[width:, :width] = total


def edge_pass(fresh, final, mix, slots, mult, src, t3, tcat, relations, relsum):
    tiles = slots // TILE
    per = tiles // mult.shape[0]
    rels, width = relations.shape
    rows, halves = tcat.shape[0], src.shape[1]

    def whole(shape):
        return pl.BlockSpec(shape, lambda i: (0,) * len(shape))

    def listed(k):
        return pl.BlockSpec((1, TILE), lambda i, k=k: (0, k * tiles + i))

    acc_at = (mix.shape[1] - LANES - halves) // halves
    count_at = mix.shape[1] // LANES - 1
    shapes = [(width + rels if final else width, rows), relsum.shape, (width + PAD, halves)]
    return pl.pallas_call(
        functools.partial(edge_kernel, fresh, final),
        grid=(tiles,),
        in_specs=[
            pl.BlockSpec((1, LANES), lambda i: (0, count_at)),
            listed(0),
            listed(1),
            listed(2),
            pl.BlockSpec((1, halves), lambda i: (0, acc_at)),
            pl.BlockSpec((1, rows, LANES), lambda i: (i // per, 0, 0)),
            whole(src.shape),
            whole(t3.shape),
            whole(tcat.shape),
            whole(relations.shape),
            whole(relsum.shape),
        ],
        out_specs=[whole(shape) for shape in shapes],
        out_shape=[jax.ShapeDtypeStruct(shape, F32) for shape in shapes],
        scratch_shapes=[
            pltpu.VMEM((width, 2 * halves), BF),
            pltpu.VMEM((width, 2 * rels), BF),
            pltpu.VMEM((width, halves), F32),
            pltpu.VMEM((width, rels), F32),
            pltpu.SMEM((1,), jnp.int32),
        ],
        compiler_params=pltpu.CompilerParams(vmem_limit_bytes=VMEM_BYTES),
        cost_estimate=CHEAP,
        name="edge_pass",
    )(mix, mix, mix, mix, mix, mult, src, t3, tcat, relations, relsum)


def update_kernel(dst_ref, state_ref, mine_ref, other_ref, dst_out, rel_out):
    width = dst_ref.shape[0]
    grad = mine_ref[:width, :] + other_ref[:width, :]
    table, state = updated(dst_ref[...], state_ref[...], grad)
    dst_out[:width, :] = table
    dst_out[width:, :] = jnp.broadcast_to(state, (PAD, state.shape[1]))
    rel_out[...] = mine_ref[width:, :width] + other_ref[width:, :width]


def final_update(dst, state, mine, other):
    width, rows = dst.shape
    return pl.pallas_call(
        update_kernel,
        out_shape=[
            jax.ShapeDtypeStruct((width + PAD, rows), F32),
            jax.ShapeDtypeStruct((mine.shape[0] - width, width), F32),
        ],
        cost_estimate=CHEAP,
        name="final_update",
    )(dst, state, mine, other)


def home(p, h, parts):
    return 2 * (p % parts) + h


def place(q, h, parts):
    q = q % parts
    return 2 * (2 * (q // 2) + h) + q % 2


def moved(value, pairs):
    return lax.ppermute(value, AXES, pairs)


def exchanged(value, bits, size):
    if len(bits) == 1:
        return value + moved(value, [(i, i ^ bits[0]) for i in range(size)])
    one, two = bits
    got = [moved(value, [(i, i ^ k) for i in range(size)]) for k in (one, two, one ^ two)]
    return (value + got[0]) + (got[1] + got[2])


def body(
    src_emb, src_acc, dst_emb, dst_acc, relations, rel_acc, edge_src, edge_dst, edge_rel, edge_counts, neg_dst
):
    parts = lax.axis_size("dom")
    rounds, slots = edge_src.shape[2:]
    blocks = neg_dst.shape[3]
    rows = dst_emb.shape[0]
    rel_edges = rounds * parts * 2 * slots // relations.shape[0]
    flat = [(p, h) for p in range(parts) for h in range(2)]

    to_place = [(home(p, h, parts), place(p, h, parts)) for p, h in flat]
    swap = [(2 * d + e, 2 * (d ^ 1) + e) for d in range(parts) for e in range(2)]
    low = 2 * (lax.axis_index("dom") % 2) + lax.axis_index("edge")
    away = jnp.where((low == 1) | (low == 2), 1, 0).reshape(1)
    dst, dst_state = dst_emb.T, dst_acc[None, :]
    other_dst, other_state = moved(dst, swap), moved(dst_state, swap)
    mixes = packed_lists(edge_src, edge_dst, edge_rel, edge_counts, neg_dst, src_acc)
    src, *mixes = lax.optimization_barrier((src_emb.T, *mixes))
    mixes = [
        moved(mix, [(home(p, h, parts), place(p - r, h, parts)) for p, h in flat]) for r, mix in enumerate(mixes)
    ]
    src = moved(src, to_place)

    relsum = jnp.zeros(relations.shape, F32)
    for r in range(rounds):
        final = r == rounds - 1
        if r == 0:
            t3, tcat, dst, dst_state = prepared(True, away, dst, other_dst, dst_state, other_state)
            t3, tcat, mix = lax.optimization_barrier((t3, tcat, mixes[0]))
        else:
            t3, tcat, dst, dst_state = prepared(False, dst, dst_state, mine, other)
            mix = mixes[r]
        mult = multiplicity(mix, 3 * slots, blocks, rows)
        if r == 0:
            src, *mixes = lax.optimization_barrier((src, *mixes))
        mine, relsum, src = edge_pass(r == 0, final, mixes[r], slots, mult, src, t3, tcat, relations, relsum)
        if not final:
            src = moved(src, [(place(p - r, h, parts), place(p - r - 1, h, parts)) for p, h in flat])
        other = moved(mine, [(place(q, h, parts), place(q, 1 - h, parts)) for q, h in flat])
    src = moved(src, [(place(p - rounds + 1, h, parts), home(p, h, parts)) for p, h in flat])
    dst, relsum = final_update(dst, dst_state, mine, other)
    dst, src = lax.optimization_barrier((dst, src))
    dst = moved(dst, [(place(q, h, parts), home(q + rounds, h, parts)) for q, h in flat])
    for bits in ((1, 4), (8, 16), (32, 64)):
        relsum = exchanged(relsum, bits, 2 * parts)
    rel_mean = relsum / rel_edges
    rel_scale = jnp.sqrt(rel_acc + jnp.mean(rel_mean * rel_mean, axis=1))
    rel_out = relations - REL_RATE * rel_mean / rel_scale[:, None]
    width = relations.shape[1]
    return (src[:width].T, src[width], dst[:width].T, dst[width], rel_out)


def solution(mesh):
    return jax.shard_map(
        body,
        mesh=mesh,
        in_specs=(
            P(("dom", "edge"), None),
            P(("dom", "edge")),
            P("dom", None),
            P("dom"),
            P(),
            P(),
            P("dom", "edge", None, None),
            P("dom", "edge", None, None),
            P("dom", "edge", None, None),
            P("dom", "edge", None),
            P("dom", "edge", None, None, None),
        ),
        out_specs=(P(("dom", "edge"), None), P(("dom", "edge")), P("dom", None), P("dom"), P()),
        check_vma=False,
    )
```

```python
import functools

import jax
import jax.numpy as jnp
from jax import lax
from jax.experimental import pallas as pl
from jax.experimental.pallas import tpu as pltpu
from jax.sharding import PartitionSpec as P

LEARN_RATE = 0.2
REL_RATE = 0.3
NEG_WEIGHT = 0.1
TILE = 256
CHUNK = 512
PAD = 8
VMEM_BYTES = 28 * 2**20
LANES = 128
BF = jnp.bfloat16
F32 = jnp.float32
CHEAP = pl.CostEstimate(flops=10**6, bytes_accessed=10**5, transcendentals=0)
AXES = ("dom", "edge")
NN = (((1,), (0,)), ((), ()))
NT = (((1,), (1,)), ((), ()))


def mm(a, b, dims=NN):
    return lax.dot_general(a, b, dims, preferred_element_type=F32)


def split(x):
    hi = x.astype(BF)
    return hi, (x - hi.astype(F32)).astype(BF)


def iota(shape, dim):
    return lax.broadcasted_iota(jnp.int32, shape, dim)


def hot(cond):
    return jnp.where(cond, F32(1), F32(0)).astype(BF)


def pack_kernel(count_ref, es_ref, ed_ref, er_ref, neg_ref, dst_acc_ref, acc_ref, *outs):
    for r, out_ref in enumerate(outs):
        parts = [es_ref[r], ed_ref[r], er_ref[r]] + [neg_ref[r, c : c + 1, :] for c in range(neg_ref.shape[1])]
        parts = [part.astype(F32) for part in parts] + [dst_acc_ref[...], acc_ref[...]]
        parts.append(jnp.full((1, LANES), count_ref[0, r], jnp.int32).astype(F32))
        out_ref[...] = jnp.concatenate(parts, axis=1)


def packed_lists(edge_src, edge_dst, edge_rel, counts, neg_dst, dst_acc, src_acc):
    rounds, slots = edge_src.shape[2:]
    size = 3 * slots + neg_dst.shape[3] * neg_dst.shape[4] + dst_acc.shape[0] + src_acc.shape[0] + LANES
    return pl.pallas_call(
        pack_kernel,
        in_specs=[pl.BlockSpec(memory_space=pltpu.SMEM)] + [pl.BlockSpec(memory_space=pltpu.VMEM)] * 6,
        out_shape=[jax.ShapeDtypeStruct((1, size), F32)] * rounds,
        compiler_params=pltpu.CompilerParams(vmem_limit_bytes=VMEM_BYTES),
        cost_estimate=CHEAP,
        name="pack_lists",
    )(
        counts.reshape(1, rounds),
        edge_src.reshape(rounds, 1, slots),
        edge_dst.reshape(rounds, 1, slots),
        edge_rel.reshape(rounds, 1, slots),
        neg_dst.reshape(neg_dst.shape[2:]),
        dst_acc.reshape(1, -1),
        src_acc.reshape(1, -1),
    )


def mult_kernel(start, mix_ref, out_ref):
    rows = out_ref.shape[1]
    high = rows // 32
    count = rows
    for c in range(out_ref.shape[0]):
        neg = mix_ref[:, start + c * count : start + (c + 1) * count].astype(jnp.int32)
        hot_hi = hot(iota((high, count), 0) == (neg >> 5))
        hot_lo = hot(iota((32, count), 0) == (neg & 31))
        counts_hi, counts_lo = split(mm(hot_hi, hot_lo, NT))
        pick = hot(iota((rows, high), 1) == (iota((rows, high), 0) >> 5))
        mask = iota((rows, 32), 1) == (iota((rows, 32), 0) & 31)
        ones = jnp.ones((32, LANES), BF)
        total = jnp.zeros((rows, LANES), F32)
        for part in (counts_hi, counts_lo):
            total += mm(jnp.where(mask, mm(pick, part), F32(0)).astype(BF), ones)
        out_ref[c] = total * (0.5 * NEG_WEIGHT)


def multiplicity(mix, start, blocks, rows):
    return pl.pallas_call(
        functools.partial(mult_kernel, start),
        out_shape=jax.ShapeDtypeStruct((blocks, rows, LANES), F32),
        compiler_params=pltpu.CompilerParams(vmem_limit_bytes=VMEM_BYTES),
        cost_estimate=CHEAP,
        name="multiplicity",
    )(mix)


def updated(table, state, grad):
    width = table.shape[0]
    new_state = state + jnp.sum(grad * grad, axis=0, keepdims=True) * F32(1.0 / width)
    return table - LEARN_RATE * grad / jnp.sqrt(new_state), new_state


def prep_kernel(fresh, state_at, *refs):
    if fresh:
        away_ref, dst_ref, other_dst_ref, t3, tcat, dst_out = refs
        dst = jnp.where(away_ref[0] > 0, other_dst_ref[...], dst_ref[...])
    else:
        dst_ref, state_ref, mine_ref, other_ref, t3, tcat, dst_out, state_out = refs
        state = state_ref[:, state_at : state_at + dst_ref.shape[1]]
        dst, state = updated(dst_ref[...], state, mine_ref[...] + other_ref[...])
        state_out[...] = state
    dst_out[...] = dst
    thi, tlo = split(dst)
    t3[...] = jnp.concatenate([thi, tlo, thi], axis=1)
    thi, tlo = thi * BF(0.5), tlo * BF(0.5)
    tcat[...] = jnp.concatenate([thi, thi, tlo], axis=0).T


def prepared(fresh, state_at, *operands):
    width, rows = operands[1].shape if fresh else operands[0].shape
    specs = [pl.BlockSpec(memory_space=pltpu.VMEM)] * len(operands)
    if fresh:
        specs[0] = pl.BlockSpec(memory_space=pltpu.SMEM)
    out_shape = [
        jax.ShapeDtypeStruct((width, 3 * rows), BF),
        jax.ShapeDtypeStruct((rows, 3 * width), BF),
        jax.ShapeDtypeStruct((width, rows), F32),
    ]
    if not fresh:
        out_shape.append(jax.ShapeDtypeStruct((1, rows), F32))
    return pl.pallas_call(
        functools.partial(prep_kernel, fresh, state_at),
        in_specs=specs,
        out_shape=out_shape,
        compiler_params=pltpu.CompilerParams(vmem_limit_bytes=VMEM_BYTES),
        cost_estimate=CHEAP,
        name="prepare_dst",
    )(*operands)


def edge_kernel(
    fresh,
    final,
    slots,
    mix_ref,
    mult_ref,
    src_ref,
    t3,
    tcat,
    rel_ref,
    relsum_ref,
    gdst,
    relsum_out,
    src_out,
    s2,
    r2,
    gsrc,
    grel,
):
    width, rows = t3.shape[0], gdst.shape[1]
    halves = gsrc.shape[1]
    rels = r2.shape[1] // 2
    per = slots // mult_ref.shape[0]
    live_count = jnp.max(mix_ref[:, mix_ref.shape[1] - LANES :]).astype(jnp.int32)
    s2[...] = jnp.concatenate(split(src_ref[:width, :]), axis=1)
    r2[...] = jnp.concatenate(split(rel_ref[...]), axis=0).T
    gsrc[...] = jnp.zeros_like(gsrc)
    gdst[...] = jnp.zeros_like(gdst)
    grel[...] = jnp.zeros_like(grel)

    def span(base, size):
        live = iota((1, size), 1) + base < live_count

        def listed(k):
            return mix_ref[:, pl.ds(pl.multiple_of(k * slots + base, TILE), size)].astype(jnp.int32)

        at = hot(iota((halves, size), 0) == jnp.where(live, listed(0), -1))
        bt = hot(iota((rels, size), 0) == jnp.where(live, listed(2), -1))
        ed = listed(1)
        sources = mm(s2[...], jnp.concatenate([at, at], axis=0))
        diag = mm(r2[...], jnp.concatenate([bt, bt], axis=0))
        qhi, qlo = split(sources * diag)
        qcat = jnp.concatenate([qhi, qlo, qhi], axis=0)
        blocks = [(base + start) // per for start in range(0, size, TILE)]
        pieces = []
        for row in range(0, rows, CHUNK):
            half = jnp.tanh(mm(tcat[row : row + CHUNK, :], qcat))
            mult = jnp.concatenate(
                [mult_ref[block, row : row + CHUNK, :] for block in blocks for _ in range(TILE // LANES)], axis=1
            )
            named = jnp.where(iota((CHUNK, size), 0) + row == ed, F32(0.5), F32(0))
            pieces.append(split(half * (mult + named) + (mult - named)))
        whi, wlo = (jnp.concatenate(piece, axis=0) for piece in zip(*pieces))
        qgrad = mm(t3[...], jnp.concatenate([whi, whi, wlo], axis=0))
        gdst[:width, :] += mm(
            jnp.concatenate([qhi, qlo, qhi], axis=1), jnp.concatenate([whi, whi, wlo], axis=1), NT
        )
        gsrc[...] += mm(
            jnp.concatenate(split(qgrad * diag), axis=1), jnp.concatenate([at, at], axis=1), NT
        )
        grel[...] += mm(
            jnp.concatenate(split(qgrad * sources), axis=1), jnp.concatenate([bt, bt], axis=1), NT
        )

    tiles = (live_count + TILE - 1) // TILE

    def two_tiles(step, _):
        span(step * 2 * TILE, 2 * TILE)
        return 0

    lax.fori_loop(0, tiles // 2, two_tiles, 0)

    @pl.when(tiles % 2 == 1)
    def _():
        span((tiles - 1) * TILE, TILE)

    state = (
        mix_ref[:, mix_ref.shape[1] - LANES - halves : mix_ref.shape[1] - LANES]
        if fresh
        else src_ref[width : width + 1, :]
    )
    table, state = updated(src_ref[:width, :], state, gsrc[...])
    src_out[:width, :] = table
    src_out[width:, :] = jnp.broadcast_to(state, (PAD, halves))
    total = relsum_ref[...] + grel[...].T
    relsum_out[...] = total
    if final:
        gdst[width:, :width] = total


def edge_pass(fresh, final, mix, slots, mult, src, t3, tcat, relations, relsum):
    rels, width = relations.shape
    rows, halves = tcat.shape[0], src.shape[1]
    shapes = [(width + rels if final else width, rows), relsum.shape, (width + PAD, halves)]
    return pl.pallas_call(
        functools.partial(edge_kernel, fresh, final, slots),
        out_shape=[jax.ShapeDtypeStruct(shape, F32) for shape in shapes],
        scratch_shapes=[
            pltpu.VMEM((width, 2 * halves), BF),
            pltpu.VMEM((width, 2 * rels), BF),
            pltpu.VMEM((width, halves), F32),
            pltpu.VMEM((width, rels), F32),
        ],
        compiler_params=pltpu.CompilerParams(vmem_limit_bytes=VMEM_BYTES),
        cost_estimate=CHEAP,
        name="edge_pass",
    )(mix, mult, src, t3, tcat, relations, relsum)


def update_kernel(dst_ref, state_ref, mine_ref, other_ref, dst_out, rel_out):
    width = dst_ref.shape[0]
    grad = mine_ref[:width, :] + other_ref[:width, :]
    table, state = updated(dst_ref[...], state_ref[...], grad)
    dst_out[:width, :] = table
    dst_out[width:, :] = jnp.broadcast_to(state, (PAD, state.shape[1]))
    rel_out[...] = mine_ref[width:, :width] + other_ref[width:, :width]


def final_update(dst, state, mine, other):
    width, rows = dst.shape
    return pl.pallas_call(
        update_kernel,
        out_shape=[
            jax.ShapeDtypeStruct((width + PAD, rows), F32),
            jax.ShapeDtypeStruct((mine.shape[0] - width, width), F32),
        ],
        compiler_params=pltpu.CompilerParams(vmem_limit_bytes=VMEM_BYTES),
        cost_estimate=CHEAP,
        name="final_update",
    )(dst, state, mine, other)


def home(p, h, parts):
    return 2 * (p % parts) + h


def place(q, h, parts):
    q = q % parts
    return 2 * (2 * (q // 2) + h) + q % 2


def moved(value, pairs):
    return lax.ppermute(value, AXES, pairs)


def exchanged(value, bits, size):
    if len(bits) == 1:
        return value + moved(value, [(i, i ^ bits[0]) for i in range(size)])
    one, two = bits
    got = [moved(value, [(i, i ^ k) for i in range(size)]) for k in (one, two, one ^ two)]
    return (value + got[0]) + (got[1] + got[2])


def body(
    src_emb, src_acc, dst_emb, dst_acc, relations, rel_acc, edge_src, edge_dst, edge_rel, edge_counts, neg_dst
):
    parts = lax.axis_size("dom")
    rounds, slots = edge_src.shape[2:]
    blocks = neg_dst.shape[3]
    rows = dst_emb.shape[0]
    rel_edges = rounds * parts * 2 * slots // relations.shape[0]
    flat = [(p, h) for p in range(parts) for h in range(2)]

    to_place = [(home(p, h, parts), place(p, h, parts)) for p, h in flat]
    swap = [(2 * d + e, 2 * (d ^ 1) + e) for d in range(parts) for e in range(2)]
    low = 2 * (lax.axis_index("dom") % 2) + lax.axis_index("edge")
    away = jnp.where((low == 1) | (low == 2), 1, 0).reshape(1)
    dst = dst_emb.T
    other_dst = moved(dst, swap)
    mixes = packed_lists(edge_src, edge_dst, edge_rel, edge_counts, neg_dst, dst_acc, src_acc)
    src, *mixes = lax.optimization_barrier((src_emb.T, *mixes))
    mixes = [
        moved(mix, [(home(p, h, parts), place(p - r, h, parts)) for p, h in flat]) for r, mix in enumerate(mixes)
    ]
    src = moved(src, to_place)

    relsum = jnp.zeros(relations.shape, F32)
    for r in range(rounds):
        final = r == rounds - 1
        if r == 0:
            t3, tcat, dst = prepared(True, 0, away, dst, other_dst)
            t3, tcat, mix = lax.optimization_barrier((t3, tcat, mixes[0]))
        else:
            state_at = 3 * slots + neg_dst.shape[3] * neg_dst.shape[4] if r == 1 else 0
            t3, tcat, dst, dst_state = prepared(
                False, state_at, dst, mixes[0] if r == 1 else dst_state, mine, other
            )
            mix = mixes[r]
        mult = multiplicity(mix, 3 * slots, blocks, rows)
        if r == 0:
            src, *mixes = lax.optimization_barrier((src, *mixes))
        mine, relsum, src = edge_pass(r == 0, final, mixes[r], slots, mult, src, t3, tcat, relations, relsum)
        if not final:
            src = moved(src, [(place(p - r, h, parts), place(p - r - 1, h, parts)) for p, h in flat])
        other = moved(mine, [(place(q, h, parts), place(q, 1 - h, parts)) for q, h in flat])
    line = parts // 16
    shift = rounds - 1
    near = [p - shift if p % line >= shift else p - shift + line for p, h in flat]
    src = moved(src, [(place(p - shift, h, parts), place(q, h, parts)) for (p, h), q in zip(flat, near)])
    dst, relsum = final_update(dst, dst_state, mine, other)
    dst = moved(dst, [(place(q, h, parts), home(q + rounds, h, parts)) for q, h in flat])
    for step, bits in enumerate(((1, 4), (8, 16), (32, 64))):
        relsum = exchanged(relsum, bits, 2 * parts)
        if step == 0:
            src, relsum = lax.optimization_barrier((src, relsum))
            src = moved(src, [(place(q, h, parts), home(p, h, parts)) for (p, h), q in zip(flat, near)])
    rel_mean = relsum / rel_edges
    rel_scale = jnp.sqrt(rel_acc + jnp.mean(rel_mean * rel_mean, axis=1))
    rel_out = relations - REL_RATE * rel_mean / rel_scale[:, None]
    width = relations.shape[1]
    return (src[:width].T, src[width], dst[:width].T, dst[width], rel_out)


def solution(mesh):
    return jax.shard_map(
        body,
        mesh=mesh,
        in_specs=(
            P(("dom", "edge"), None),
            P(("dom", "edge")),
            P("dom", None),
            P("dom"),
            P(),
            P(),
            P("dom", "edge", None, None),
            P("dom", "edge", None, None),
            P("dom", "edge", None, None),
            P("dom", "edge", None),
            P("dom", "edge", None, None, None),
        ),
        out_specs=(P(("dom", "edge"), None), P(("dom", "edge")), P("dom", None), P("dom"), P()),
        check_vma=False,
    )
```

```python
import functools

import jax
import jax.numpy as jnp
from jax import lax
from jax.experimental import pallas as pl
from jax.experimental.pallas import tpu as pltpu
from jax.sharding import PartitionSpec as P

LEARN_RATE = 0.2
REL_RATE = 0.3
NEG_WEIGHT = 0.1
TILE = 256
CHUNK = 512
PAD = 8
VMEM_BYTES = 28 * 2**20
LANES = 128
BF = jnp.bfloat16
F32 = jnp.float32
CHEAP = pl.CostEstimate(flops=10**6, bytes_accessed=10**5, transcendentals=0)
AXES = ("dom", "edge")
NN = (((1,), (0,)), ((), ()))
NT = (((1,), (1,)), ((), ()))


def mm(a, b, dims=NN):
    return lax.dot_general(a, b, dims, preferred_element_type=F32)


def split(x):
    hi = x.astype(BF)
    return hi, (x - hi.astype(F32)).astype(BF)


def iota(shape, dim):
    return lax.broadcasted_iota(jnp.int32, shape, dim)


def hot(cond):
    return jnp.where(cond, F32(1), F32(0)).astype(BF)


def pack_kernel(count_ref, es_ref, ed_ref, er_ref, neg_ref, dst_acc_ref, acc_ref, *outs):
    for r, out_ref in enumerate(outs):
        parts = [es_ref[r], ed_ref[r], er_ref[r]] + [neg_ref[r, c : c + 1, :] for c in range(neg_ref.shape[1])]
        parts = [part.astype(F32) for part in parts] + [dst_acc_ref[...], acc_ref[...]]
        parts.append(jnp.full((1, LANES), count_ref[0, r], jnp.int32).astype(F32))
        out_ref[...] = jnp.concatenate(parts, axis=1)


def packed_lists(edge_src, edge_dst, edge_rel, counts, neg_dst, dst_acc, src_acc):
    rounds, slots = edge_src.shape[2:]
    size = 3 * slots + neg_dst.shape[3] * neg_dst.shape[4] + dst_acc.shape[0] + src_acc.shape[0] + LANES
    return pl.pallas_call(
        pack_kernel,
        in_specs=[pl.BlockSpec(memory_space=pltpu.SMEM)] + [pl.BlockSpec(memory_space=pltpu.VMEM)] * 6,
        out_shape=[jax.ShapeDtypeStruct((1, size), F32)] * rounds,
        compiler_params=pltpu.CompilerParams(vmem_limit_bytes=2 * VMEM_BYTES),
        cost_estimate=CHEAP,
        name="pack_lists",
    )(
        counts.reshape(1, rounds),
        edge_src.reshape(rounds, 1, slots),
        edge_dst.reshape(rounds, 1, slots),
        edge_rel.reshape(rounds, 1, slots),
        neg_dst.reshape(neg_dst.shape[2:]),
        dst_acc.reshape(1, -1),
        src_acc.reshape(1, -1),
    )


def mult_kernel(start, mix_ref, out_ref):
    rows = out_ref.shape[1]
    high = rows // 32
    count = rows
    for c in range(out_ref.shape[0]):
        neg = mix_ref[:, start + c * count : start + (c + 1) * count].astype(jnp.int32)
        hot_hi = hot(iota((high, count), 0) == (neg >> 5))
        hot_lo = hot(iota((32, count), 0) == (neg & 31))
        counts_hi, counts_lo = split(mm(hot_hi, hot_lo, NT))
        pick = hot(iota((rows, high), 1) == (iota((rows, high), 0) >> 5))
        mask = iota((rows, 32), 1) == (iota((rows, 32), 0) & 31)
        ones = jnp.ones((32, LANES), BF)
        total = jnp.zeros((rows, LANES), F32)
        for part in (counts_hi, counts_lo):
            total += mm(jnp.where(mask, mm(pick, part), F32(0)).astype(BF), ones)
        out_ref[c] = total * (0.5 * NEG_WEIGHT)


def multiplicity(mix, start, blocks, rows):
    return pl.pallas_call(
        functools.partial(mult_kernel, start),
        out_shape=jax.ShapeDtypeStruct((blocks, rows, LANES), F32),
        compiler_params=pltpu.CompilerParams(vmem_limit_bytes=VMEM_BYTES),
        cost_estimate=CHEAP,
        name="multiplicity",
    )(mix)


def updated(table, state, grad):
    width = table.shape[0]
    new_state = state + jnp.sum(grad * grad, axis=0, keepdims=True) * F32(1.0 / width)
    return table - LEARN_RATE * grad / jnp.sqrt(new_state), new_state


def prep_kernel(fresh, state_at, *refs):
    if fresh:
        away_ref, dst_ref, other_dst_ref, t3, tcat, dst_out = refs
        dst = jnp.where(away_ref[0] > 0, other_dst_ref[...], dst_ref[...])
    else:
        dst_ref, state_ref, mine_ref, other_ref, t3, tcat, dst_out, state_out = refs
        state = state_ref[:, state_at : state_at + dst_ref.shape[1]]
        dst, state = updated(dst_ref[...], state, mine_ref[...] + other_ref[...])
        state_out[...] = state
    dst_out[...] = dst
    thi, tlo = split(dst)
    t3[...] = jnp.concatenate([thi, tlo, thi], axis=1)
    thi, tlo = thi * BF(0.5), tlo * BF(0.5)
    tcat[...] = jnp.concatenate([thi, thi, tlo], axis=0).T


def prepared(fresh, state_at, *operands):
    width, rows = operands[1].shape if fresh else operands[0].shape
    specs = [pl.BlockSpec(memory_space=pltpu.VMEM)] * len(operands)
    if fresh:
        specs[0] = pl.BlockSpec(memory_space=pltpu.SMEM)
    out_shape = [
        jax.ShapeDtypeStruct((width, 3 * rows), BF),
        jax.ShapeDtypeStruct((rows, 3 * width), BF),
        jax.ShapeDtypeStruct((width, rows), F32),
    ]
    if not fresh:
        out_shape.append(jax.ShapeDtypeStruct((1, rows), F32))
    return pl.pallas_call(
        functools.partial(prep_kernel, fresh, state_at),
        in_specs=specs,
        out_shape=out_shape,
        compiler_params=pltpu.CompilerParams(vmem_limit_bytes=VMEM_BYTES),
        cost_estimate=CHEAP,
        name="prepare_dst",
    )(*operands)


def edge_kernel(
    fresh,
    final,
    slots,
    mix_ref,
    mult_ref,
    src_ref,
    t3,
    tcat,
    rel_ref,
    relsum_ref,
    gdst,
    relsum_out,
    src_out,
    s2,
    r2,
    gsrc,
    grel,
):
    width, rows = t3.shape[0], gdst.shape[1]
    halves = gsrc.shape[1]
    rels = r2.shape[1] // 2
    per = slots // mult_ref.shape[0]
    live_count = jnp.max(mix_ref[:, mix_ref.shape[1] - LANES :]).astype(jnp.int32)
    s2[...] = jnp.concatenate(split(src_ref[:width, :]), axis=1)
    r2[...] = jnp.concatenate(split(rel_ref[...]), axis=0).T
    gsrc[...] = jnp.zeros_like(gsrc)
    gdst[...] = jnp.zeros_like(gdst)
    grel[...] = jnp.zeros_like(grel)

    def span(base, size):
        live = iota((1, size), 1) + base < live_count

        def listed(k):
            return mix_ref[:, pl.ds(pl.multiple_of(k * slots + base, TILE), size)].astype(jnp.int32)

        at = hot(iota((halves, size), 0) == jnp.where(live, listed(0), -1))
        bt = hot(iota((rels, size), 0) == jnp.where(live, listed(2), -1))
        ed = listed(1)
        sources = mm(s2[...], jnp.concatenate([at, at], axis=0))
        diag = mm(r2[...], jnp.concatenate([bt, bt], axis=0))
        qhi, qlo = split(sources * diag)
        qcat = jnp.concatenate([qhi, qlo, qhi], axis=0)
        blocks = [(base + start) // per for start in range(0, size, TILE)]
        pieces = []
        for row in range(0, rows, CHUNK):
            half = jnp.tanh(mm(tcat[row : row + CHUNK, :], qcat))
            mult = jnp.concatenate(
                [mult_ref[block, row : row + CHUNK, :] for block in blocks for _ in range(TILE // LANES)], axis=1
            )
            named = jnp.where(iota((CHUNK, size), 0) + row == ed, F32(0.5), F32(0))
            pieces.append(split(half * (mult + named) + (mult - named)))
        whi, wlo = (jnp.concatenate(piece, axis=0) for piece in zip(*pieces))
        qgrad = mm(t3[...], jnp.concatenate([whi, whi, wlo], axis=0))
        gdst[:width, :] += mm(
            jnp.concatenate([qhi, qlo, qhi], axis=1), jnp.concatenate([whi, whi, wlo], axis=1), NT
        )
        gsrc[...] += mm(
            jnp.concatenate(split(qgrad * diag), axis=1), jnp.concatenate([at, at], axis=1), NT
        )
        grel[...] += mm(
            jnp.concatenate(split(qgrad * sources), axis=1), jnp.concatenate([bt, bt], axis=1), NT
        )

    tiles = (live_count + TILE - 1) // TILE
    rest = tiles % 3

    def three_tiles(step, _):
        span(step * 3 * TILE, 3 * TILE)
        return 0

    lax.fori_loop(0, tiles // 3, three_tiles, 0)

    @pl.when(rest == 2)
    def _():
        span((tiles - 2) * TILE, 2 * TILE)

    @pl.when(rest == 1)
    def _():
        span((tiles - 1) * TILE, TILE)

    state = (
        mix_ref[:, mix_ref.shape[1] - LANES - halves : mix_ref.shape[1] - LANES]
        if fresh
        else src_ref[width : width + 1, :]
    )
    table, state = updated(src_ref[:width, :], state, gsrc[...])
    src_out[:width, :] = table
    src_out[width:, :] = jnp.broadcast_to(state, (PAD, halves))
    total = relsum_ref[...] + grel[...].T
    relsum_out[...] = total
    if final:
        gdst[width:, :width] = total


def edge_pass(fresh, final, mix, slots, mult, src, t3, tcat, relations, relsum):
    rels, width = relations.shape
    rows, halves = tcat.shape[0], src.shape[1]
    shapes = [(width + rels if final else width, rows), relsum.shape, (width + PAD, halves)]
    return pl.pallas_call(
        functools.partial(edge_kernel, fresh, final, slots),
        out_shape=[jax.ShapeDtypeStruct(shape, F32) for shape in shapes],
        scratch_shapes=[
            pltpu.VMEM((width, 2 * halves), BF),
            pltpu.VMEM((width, 2 * rels), BF),
            pltpu.VMEM((width, halves), F32),
            pltpu.VMEM((width, rels), F32),
        ],
        compiler_params=pltpu.CompilerParams(vmem_limit_bytes=VMEM_BYTES),
        cost_estimate=CHEAP,
        name="edge_pass",
    )(mix, mult, src, t3, tcat, relations, relsum)


def update_kernel(dst_ref, state_ref, mine_ref, other_ref, dst_out, rel_out):
    width = dst_ref.shape[0]
    grad = mine_ref[:width, :] + other_ref[:width, :]
    table, state = updated(dst_ref[...], state_ref[...], grad)
    dst_out[:width, :] = table
    dst_out[width:, :] = jnp.broadcast_to(state, (PAD, state.shape[1]))
    rel_out[...] = mine_ref[width:, :width] + other_ref[width:, :width]


def final_update(dst, state, mine, other):
    width, rows = dst.shape
    return pl.pallas_call(
        update_kernel,
        out_shape=[
            jax.ShapeDtypeStruct((width + PAD, rows), F32),
            jax.ShapeDtypeStruct((mine.shape[0] - width, width), F32),
        ],
        compiler_params=pltpu.CompilerParams(vmem_limit_bytes=VMEM_BYTES),
        cost_estimate=CHEAP,
        name="final_update",
    )(dst, state, mine, other)


def home(p, h, parts):
    return 2 * (p % parts) + h


def place(q, h, parts):
    q = q % parts
    return 2 * (2 * (q // 2) + h) + q % 2


def moved(value, pairs):
    return lax.ppermute(value, AXES, pairs)


def exchanged(value, bits, size):
    if len(bits) == 1:
        return value + moved(value, [(i, i ^ bits[0]) for i in range(size)])
    one, two = bits
    got = [moved(value, [(i, i ^ k) for i in range(size)]) for k in (one, two, one ^ two)]
    return (value + got[0]) + (got[1] + got[2])


def body(
    src_emb, src_acc, dst_emb, dst_acc, relations, rel_acc, edge_src, edge_dst, edge_rel, edge_counts, neg_dst
):
    parts = lax.axis_size("dom")
    rounds, slots = edge_src.shape[2:]
    blocks = neg_dst.shape[3]
    rows = dst_emb.shape[0]
    rel_edges = rounds * parts * 2 * slots // relations.shape[0]
    flat = [(p, h) for p in range(parts) for h in range(2)]

    to_place = [(home(p, h, parts), place(p, h, parts)) for p, h in flat]
    swap = [(2 * d + e, 2 * (d ^ 1) + e) for d in range(parts) for e in range(2)]
    low = 2 * (lax.axis_index("dom") % 2) + lax.axis_index("edge")
    away = jnp.where((low == 1) | (low == 2), 1, 0).reshape(1)
    dst = dst_emb.T
    other_dst = moved(dst, swap)
    mixes = packed_lists(edge_src, edge_dst, edge_rel, edge_counts, neg_dst, dst_acc, src_acc)
    src, *mixes = lax.optimization_barrier((src_emb.T, *mixes))
    mixes = [
        moved(mix, [(home(p, h, parts), place(p - r, h, parts)) for p, h in flat]) for r, mix in enumerate(mixes)
    ]
    src = moved(src, to_place)

    relsum = jnp.zeros(relations.shape, F32)
    for r in range(rounds):
        final = r == rounds - 1
        if r == 0:
            t3, tcat, dst = prepared(True, 0, away, dst, other_dst)
            t3, tcat, mix = lax.optimization_barrier((t3, tcat, mixes[0]))
        else:
            state_at = 3 * slots + neg_dst.shape[3] * neg_dst.shape[4] if r == 1 else 0
            t3, tcat, dst, dst_state = prepared(
                False, state_at, dst, mixes[0] if r == 1 else dst_state, mine, other
            )
            mix = mixes[r]
        mult = multiplicity(mix, 3 * slots, blocks, rows)
        if r == 0:
            src, *mixes = lax.optimization_barrier((src, *mixes))
        mine, relsum, src = edge_pass(r == 0, final, mixes[r], slots, mult, src, t3, tcat, relations, relsum)
        if not final:
            src = moved(src, [(place(p - r, h, parts), place(p - r - 1, h, parts)) for p, h in flat])
        other = moved(mine, [(place(q, h, parts), place(q, 1 - h, parts)) for q, h in flat])
    line = parts // 16
    shift = rounds - 1
    near = [p - shift if p % line >= shift else p - shift + line for p, h in flat]
    src = moved(src, [(place(p - shift, h, parts), place(q, h, parts)) for (p, h), q in zip(flat, near)])
    dst, relsum = final_update(dst, dst_state, mine, other)
    dst = moved(dst, [(place(q, h, parts), home(q + rounds, h, parts)) for q, h in flat])
    for step, bits in enumerate(((1, 4), (8, 16), (32, 64))):
        relsum = exchanged(relsum, bits, 2 * parts)
        if step == 0:
            src, _ = lax.optimization_barrier((src, relsum))
            src = moved(src, [(place(q, h, parts), home(p, h, parts)) for (p, h), q in zip(flat, near)])
    rel_mean = relsum / rel_edges
    rel_scale = jnp.sqrt(rel_acc + jnp.mean(rel_mean * rel_mean, axis=1))
    rel_out = relations - REL_RATE * rel_mean / rel_scale[:, None]
    width = relations.shape[1]
    return (src[:width].T, src[width], dst[:width].T, dst[width], rel_out)


def solution(mesh):
    return jax.shard_map(
        body,
        mesh=mesh,
        in_specs=(
            P(("dom", "edge"), None),
            P(("dom", "edge")),
            P("dom", None),
            P("dom"),
            P(),
            P(),
            P("dom", "edge", None, None),
            P("dom", "edge", None, None),
            P("dom", "edge", None, None),
            P("dom", "edge", None),
            P("dom", "edge", None, None, None),
        ),
        out_specs=(P(("dom", "edge"), None), P(("dom", "edge")), P("dom", None), P("dom"), P()),
        check_vma=False,
    )
```

```python
import functools

import jax
import jax.numpy as jnp
from jax import lax
from jax.experimental import pallas as pl
from jax.experimental.pallas import tpu as pltpu
from jax.sharding import PartitionSpec as P

LEARN_RATE = 0.2
REL_RATE = 0.3
NEG_WEIGHT = 0.1
TILE = 256
CHUNK = 512
PAD = 8
VMEM_BYTES = 22 * 2**20
LANES = 128
BF = jnp.bfloat16
F32 = jnp.float32
CHEAP = pl.CostEstimate(flops=10**6, bytes_accessed=10**5, transcendentals=0)
AXES = ("dom", "edge")
NN = (((1,), (0,)), ((), ()))
NT = (((1,), (1,)), ((), ()))


def mm(a, b, dims=NN):
    return lax.dot_general(a, b, dims, preferred_element_type=F32)


def split(x):
    hi = x.astype(BF)
    return hi, (x - hi.astype(F32)).astype(BF)


def iota(shape, dim):
    return lax.broadcasted_iota(jnp.int32, shape, dim)


def hot(cond):
    return jnp.where(cond, F32(1), F32(0)).astype(BF)


def pack_kernel(count_ref, es_ref, ed_ref, er_ref, neg_ref, dst_acc_ref, acc_ref, *outs):
    for r, out_ref in enumerate(outs):
        parts = [es_ref[r], ed_ref[r], er_ref[r]] + [neg_ref[r, c : c + 1, :] for c in range(neg_ref.shape[1])]
        parts = [part.astype(F32) for part in parts] + [dst_acc_ref[...], acc_ref[...]]
        parts.append(jnp.full((1, LANES), count_ref[0, r], jnp.int32).astype(F32))
        out_ref[...] = jnp.concatenate(parts, axis=1)


def packed_lists(edge_src, edge_dst, edge_rel, counts, neg_dst, dst_acc, src_acc):
    rounds, slots = edge_src.shape[2:]
    size = 3 * slots + neg_dst.shape[3] * neg_dst.shape[4] + dst_acc.shape[0] + src_acc.shape[0] + LANES
    return pl.pallas_call(
        pack_kernel,
        in_specs=[pl.BlockSpec(memory_space=pltpu.SMEM)] + [pl.BlockSpec(memory_space=pltpu.VMEM)] * 6,
        out_shape=[jax.ShapeDtypeStruct((1, size), F32)] * rounds,
        compiler_params=pltpu.CompilerParams(vmem_limit_bytes=56 * 2**20),
        cost_estimate=CHEAP,
        name="pack_lists",
    )(
        counts.reshape(1, rounds),
        edge_src.reshape(rounds, 1, slots),
        edge_dst.reshape(rounds, 1, slots),
        edge_rel.reshape(rounds, 1, slots),
        neg_dst.reshape(neg_dst.shape[2:]),
        dst_acc.reshape(1, -1),
        src_acc.reshape(1, -1),
    )


def mult_kernel(start, mix_ref, out_ref):
    rows = out_ref.shape[1]
    high = rows // 32
    count = rows
    for c in range(out_ref.shape[0]):
        neg = mix_ref[:, start + c * count : start + (c + 1) * count].astype(jnp.int32)
        hot_hi = hot(iota((high, count), 0) == (neg >> 5))
        hot_lo = hot(iota((32, count), 0) == (neg & 31))
        counts_hi, counts_lo = split(mm(hot_hi, hot_lo, NT))
        pick = hot(iota((rows, high), 1) == (iota((rows, high), 0) >> 5))
        mask = iota((rows, 32), 1) == (iota((rows, 32), 0) & 31)
        ones = jnp.ones((32, LANES), BF)
        total = jnp.zeros((rows, LANES), F32)
        for part in (counts_hi, counts_lo):
            total += mm(jnp.where(mask, mm(pick, part), F32(0)).astype(BF), ones)
        out_ref[c] = total * (0.5 * NEG_WEIGHT)


def multiplicity(mix, start, blocks, rows):
    return pl.pallas_call(
        functools.partial(mult_kernel, start),
        out_shape=jax.ShapeDtypeStruct((blocks, rows, LANES), F32),
        compiler_params=pltpu.CompilerParams(vmem_limit_bytes=VMEM_BYTES),
        cost_estimate=CHEAP,
        name="multiplicity",
    )(mix)


def updated(table, state, grad):
    width = table.shape[0]
    new_state = state + jnp.sum(grad * grad, axis=0, keepdims=True) * F32(1.0 / width)
    return table - LEARN_RATE * grad / jnp.sqrt(new_state), new_state


def prep_kernel(fresh, state_at, *refs):
    if fresh:
        away_ref, dst_ref, other_dst_ref, t3, tcat, dst_out = refs
        dst = jnp.where(away_ref[0] > 0, other_dst_ref[...], dst_ref[...])
    else:
        dst_ref, state_ref, mine_ref, other_ref, t3, tcat, dst_out, state_out = refs
        state = state_ref[:, state_at : state_at + dst_ref.shape[1]]
        dst, state = updated(dst_ref[...], state, mine_ref[...] + other_ref[...])
        state_out[...] = state
    dst_out[...] = dst
    thi, tlo = split(dst)
    t3[...] = jnp.concatenate([thi, tlo, thi], axis=1)
    thi, tlo = thi * BF(0.5), tlo * BF(0.5)
    tcat[...] = jnp.concatenate([thi, thi, tlo], axis=0).T


def prepared(fresh, state_at, *operands):
    width, rows = operands[1].shape if fresh else operands[0].shape
    specs = [pl.BlockSpec(memory_space=pltpu.VMEM)] * len(operands)
    if fresh:
        specs[0] = pl.BlockSpec(memory_space=pltpu.SMEM)
    out_shape = [
        jax.ShapeDtypeStruct((width, 3 * rows), BF),
        jax.ShapeDtypeStruct((rows, 3 * width), BF),
        jax.ShapeDtypeStruct((width, rows), F32),
    ]
    if not fresh:
        out_shape.append(jax.ShapeDtypeStruct((1, rows), F32))
    return pl.pallas_call(
        functools.partial(prep_kernel, fresh, state_at),
        in_specs=specs,
        out_shape=out_shape,
        compiler_params=pltpu.CompilerParams(vmem_limit_bytes=VMEM_BYTES),
        cost_estimate=CHEAP,
        name="prepare_dst",
    )(*operands)


def edge_kernel(
    fresh,
    final,
    slots,
    mix_ref,
    mult_ref,
    src_ref,
    t3,
    tcat,
    rel_ref,
    relsum_ref,
    gdst,
    relsum_out,
    src_out,
    s2,
    r2,
    gsrc,
    grel,
):
    width, rows = t3.shape[0], gdst.shape[1]
    halves = gsrc.shape[1]
    rels = r2.shape[1] // 2
    per = slots // mult_ref.shape[0]
    live_count = jnp.max(mix_ref[:, mix_ref.shape[1] - LANES :]).astype(jnp.int32)
    s2[...] = jnp.concatenate(split(src_ref[:width, :]), axis=1)
    r2[...] = jnp.concatenate(split(rel_ref[...]), axis=0).T
    gsrc[...] = jnp.zeros_like(gsrc)
    gdst[...] = jnp.zeros_like(gdst)
    grel[...] = jnp.zeros_like(grel)

    def span(base, size):
        live = iota((1, size), 1) + base < live_count

        def listed(k):
            return mix_ref[:, pl.ds(pl.multiple_of(k * slots + base, TILE), size)].astype(jnp.int32)

        at = hot(iota((halves, size), 0) == jnp.where(live, listed(0), -1))
        bt = hot(iota((rels, size), 0) == jnp.where(live, listed(2), -1))
        ed = listed(1)
        sources = mm(s2[...], jnp.concatenate([at, at], axis=0))
        diag = mm(r2[...], jnp.concatenate([bt, bt], axis=0))
        qhi, qlo = split(sources * diag)
        qcat = jnp.concatenate([qhi, qlo, qhi], axis=0)
        blocks = [(base + start) // per for start in range(0, size, TILE)]
        pieces = []
        for row in range(0, rows, CHUNK):
            half = jnp.tanh(mm(tcat[row : row + CHUNK, :], qcat))
            mult = jnp.concatenate(
                [mult_ref[block, row : row + CHUNK, :] for block in blocks for _ in range(TILE // LANES)], axis=1
            )
            named = jnp.where(iota((CHUNK, size), 0) + row == ed, F32(0.5), F32(0))
            pieces.append(split(half * (mult + named) + (mult - named)))
        whi, wlo = (jnp.concatenate(piece, axis=0) for piece in zip(*pieces))
        qgrad = mm(t3[...], jnp.concatenate([whi, whi, wlo], axis=0))
        gdst[:width, :] += mm(
            jnp.concatenate([qhi, qlo, qhi], axis=1), jnp.concatenate([whi, whi, wlo], axis=1), NT
        )
        gsrc[...] += mm(
            jnp.concatenate(split(qgrad * diag), axis=1), jnp.concatenate([at, at], axis=1), NT
        )
        grel[...] += mm(
            jnp.concatenate(split(qgrad * sources), axis=1), jnp.concatenate([bt, bt], axis=1), NT
        )

    tiles = (live_count + TILE - 1) // TILE
    rest = tiles % 3

    def three_tiles(step, _):
        span(step * 3 * TILE, 3 * TILE)
        return 0

    lax.fori_loop(0, tiles // 3, three_tiles, 0)

    @pl.when(rest == 2)
    def _():
        span((tiles - 2) * TILE, 2 * TILE)

    @pl.when(rest == 1)
    def _():
        span((tiles - 1) * TILE, TILE)

    state = (
        mix_ref[:, mix_ref.shape[1] - LANES - halves : mix_ref.shape[1] - LANES]
        if fresh
        else src_ref[width : width + 1, :]
    )
    table, state = updated(src_ref[:width, :], state, gsrc[...])
    src_out[:width, :] = table
    src_out[width:, :] = jnp.broadcast_to(state, (PAD, halves))
    total = relsum_ref[...] + grel[...].T
    relsum_out[...] = total
    if final:
        gdst[width:, :width] = total


def edge_pass(fresh, final, mix, slots, mult, src, t3, tcat, relations, relsum):
    rels, width = relations.shape
    rows, halves = tcat.shape[0], src.shape[1]
    shapes = [(width + rels if final else width, rows), relsum.shape, (width + PAD, halves)]
    return pl.pallas_call(
        functools.partial(edge_kernel, fresh, final, slots),
        out_shape=[jax.ShapeDtypeStruct(shape, F32) for shape in shapes],
        scratch_shapes=[
            pltpu.VMEM((width, 2 * halves), BF),
            pltpu.VMEM((width, 2 * rels), BF),
            pltpu.VMEM((width, halves), F32),
            pltpu.VMEM((width, rels), F32),
        ],
        compiler_params=pltpu.CompilerParams(vmem_limit_bytes=VMEM_BYTES),
        cost_estimate=CHEAP,
        name="edge_pass",
    )(mix, mult, src, t3, tcat, relations, relsum)


def update_kernel(dst_ref, state_ref, mine_ref, other_ref, dst_out, rel_out):
    width = dst_ref.shape[0]
    grad = mine_ref[:width, :] + other_ref[:width, :]
    table, state = updated(dst_ref[...], state_ref[...], grad)
    dst_out[:width, :] = table
    dst_out[width:, :] = jnp.broadcast_to(state, (PAD, state.shape[1]))
    rel_out[...] = mine_ref[width:, :width] + other_ref[width:, :width]


def final_update(dst, state, mine, other):
    width, rows = dst.shape
    return pl.pallas_call(
        update_kernel,
        out_shape=[
            jax.ShapeDtypeStruct((width + PAD, rows), F32),
            jax.ShapeDtypeStruct((mine.shape[0] - width, width), F32),
        ],
        compiler_params=pltpu.CompilerParams(vmem_limit_bytes=VMEM_BYTES),
        cost_estimate=CHEAP,
        name="final_update",
    )(dst, state, mine, other)


def home(p, h, parts):
    return 2 * (p % parts) + h


def place(q, h, parts):
    q = q % parts
    return 2 * (2 * (q // 2) + h) + q % 2


def moved(value, pairs):
    return lax.ppermute(value, AXES, pairs)


def exchanged(value, bits, size):
    if len(bits) == 1:
        return value + moved(value, [(i, i ^ bits[0]) for i in range(size)])
    one, two = bits
    got = [moved(value, [(i, i ^ k) for i in range(size)]) for k in (one, two, one ^ two)]
    return (value + got[0]) + (got[1] + got[2])


def body(
    src_emb, src_acc, dst_emb, dst_acc, relations, rel_acc, edge_src, edge_dst, edge_rel, edge_counts, neg_dst
):
    parts = lax.axis_size("dom")
    rounds, slots = edge_src.shape[2:]
    blocks = neg_dst.shape[3]
    rows = dst_emb.shape[0]
    rel_edges = rounds * parts * 2 * slots // relations.shape[0]
    flat = [(p, h) for p in range(parts) for h in range(2)]

    to_place = [(home(p, h, parts), place(p, h, parts)) for p, h in flat]
    swap = [(2 * d + e, 2 * (d ^ 1) + e) for d in range(parts) for e in range(2)]
    low = 2 * (lax.axis_index("dom") % 2) + lax.axis_index("edge")
    away = jnp.where((low == 1) | (low == 2), 1, 0).reshape(1)
    dst = dst_emb.T
    other_dst = moved(dst, swap)
    mixes = packed_lists(edge_src, edge_dst, edge_rel, edge_counts, neg_dst, dst_acc, src_acc)
    src, *mixes = lax.optimization_barrier((src_emb.T, *mixes))
    mixes = [
        moved(mix, [(home(p, h, parts), place(p - r, h, parts)) for p, h in flat]) for r, mix in enumerate(mixes)
    ]
    src = moved(src, to_place)

    relsum = jnp.zeros(relations.shape, F32)
    for r in range(rounds):
        final = r == rounds - 1
        if r == 0:
            t3, tcat, dst = prepared(True, 0, away, dst, other_dst)
            t3, tcat, mix = lax.optimization_barrier((t3, tcat, mixes[0]))
        else:
            state_at = 3 * slots + neg_dst.shape[3] * neg_dst.shape[4] if r == 1 else 0
            t3, tcat, dst, dst_state = prepared(
                False, state_at, dst, mixes[0] if r == 1 else dst_state, mine, other
            )
            mix = mixes[r]
        mult = multiplicity(mix, 3 * slots, blocks, rows)
        if r == 0:
            src, *mixes = lax.optimization_barrier((src, *mixes))
        mine, relsum, src = edge_pass(r == 0, final, mixes[r], slots, mult, src, t3, tcat, relations, relsum)
        if not final:
            src = moved(src, [(place(p - r, h, parts), place(p - r - 1, h, parts)) for p, h in flat])
        other = moved(mine, [(place(q, h, parts), place(q, 1 - h, parts)) for q, h in flat])
    line = parts // 16
    shift = rounds - 1
    near = [p - shift if p % line >= shift else p - shift + line for p, h in flat]
    src = moved(src, [(place(p - shift, h, parts), place(q, h, parts)) for (p, h), q in zip(flat, near)])
    dst, relsum = final_update(dst, dst_state, mine, other)
    dst = moved(dst, [(place(q, h, parts), home(q + rounds, h, parts)) for q, h in flat])
    for step, bits in enumerate(((1, 4), (8, 16), (32, 64))):
        relsum = exchanged(relsum, bits, 2 * parts)
        if step == 0:
            src, _ = lax.optimization_barrier((src, relsum))
            src = moved(src, [(place(q, h, parts), home(p, h, parts)) for (p, h), q in zip(flat, near)])
    rel_mean = relsum / rel_edges
    rel_scale = jnp.sqrt(rel_acc + jnp.mean(rel_mean * rel_mean, axis=1))
    rel_out = relations - REL_RATE * rel_mean / rel_scale[:, None]
    width = relations.shape[1]
    return (src[:width].T, src[width], dst[:width].T, dst[width], rel_out)


def solution(mesh):
    return jax.shard_map(
        body,
        mesh=mesh,
        in_specs=(
            P(("dom", "edge"), None),
            P(("dom", "edge")),
            P("dom", None),
            P("dom"),
            P(),
            P(),
            P("dom", "edge", None, None),
            P("dom", "edge", None, None),
            P("dom", "edge", None, None),
            P("dom", "edge", None),
            P("dom", "edge", None, None, None),
        ),
        out_specs=(P(("dom", "edge"), None), P(("dom", "edge")), P("dom", None), P("dom"), P()),
        check_vma=False,
    )
```
